256 devices in a mesh: prow: 32 (over z_hi, x, y), pcol: 8 (over z_lo, core).
Axes of the slice: x: 4, y: 4, z: 8 (z_hi: 2, z_lo: 4; z = z_hi * 4 + z_lo), core: 2. Of those that a mesh axis runs over, the one named last changes fastest.
Arguments:
- inverse: bfloat16 [2, 4096, 4096], P(None, 'pcol', 'prow'), may hold values from -0.09375 to 0.09375
- coupling: bfloat16 [4096, 4096], P('prow', 'pcol'), may hold values from -0.09375 to 0.09375
- panel: bfloat16 [2, 49152, 4096], P(None, 'prow', 'pcol'), may hold values from -0.0625 to 0.0625
- modes: bfloat16 [2, 512, 4096], P(None, 'prow', 'pcol'), may hold values from -0.0625 to 0.0625
- rhs_window: bfloat16 [2, 4096, 1024], P(None, ('prow', 'pcol')), may hold values from -6 to 6
- rhs_above: bfloat16 [49152, 1024], P(('prow', 'pcol')), may hold values from -6 to 6
Outputs:
- potential: bfloat16 [2, 4096, 1024], P(None, ('pcol', 'prow'))
- above_rows: float32 [49152, 1024], P(('prow', 'pcol'))
- forces: float32 [512, 1024], P(('prow', 'pcol'))
The draws below stay inside these ranges and needn't reach their ends.
All inputs are finite; a program needn't handle non-finite values.
Results may differ from the reference program's by a relative error of at most 0.02.
Values may be sent and summed in bfloat16 or wider, within the bound.
A program may use at most 64 MiB of HBM per device.

```python
import jax
import jax.numpy as jnp
from jax import lax

NB = 4096
RHS = 1024
MODES = 512
ABOVE = 49152


def block_levels(stream_key, shape, cuts, least, high):
    def one(dim, shards_of):
        draws = jax.random.uniform(jax.random.fold_in(jax.random.fold_in(stream_key, 6), dim), (shards_of,), jnp.float32, least / len(cuts), high / len(cuts))
        return jnp.repeat(jnp.exp(draws), shape[dim] // shards_of).reshape((-1,) + (1,) * (len(shape) - dim - 1))

    level = one(*cuts[0])
    for cut in cuts[1:]:
        level = level * one(*cut)
    return level


def bell_draw(rng, shape, spread, reach, pieces=(), dtype=jnp.bfloat16):
    loudness = block_levels(rng, shape, pieces, -0.22, 0.18) if pieces else 1.0
    result = jax.random.normal(rng, shape, jnp.float32) * spread * loudness
    return jnp.minimum(jnp.maximum(result, -reach), reach).astype(dtype)


def setup_inputs(seed: int = 0) -> dict:
    key_list = jax.random.split(jax.random.key(seed), 7)
    return {
        "inverse": bell_draw(key_list[0], (2, NB, NB), NB ** -0.5, 0.09375, ((1, 8), (2, 32))),
        "coupling": bell_draw(key_list[1], (NB, NB), NB ** -0.5, 0.09375, ((0, 32), (1, 8))),
        "panel": bell_draw(key_list[2], (2, ABOVE, NB), (2 * NB) ** -0.5, 0.0625, ((1, 32), (2, 8))),
        "modes": bell_draw(key_list[3], (2, MODES, NB), (2 * NB) ** -0.5, 0.0625, ((1, 32), (2, 8))),
        "rhs_window": bell_draw(key_list[4], (2, NB, RHS), 1.0, 6.0, ((1, 256),)),
        "rhs_above": bell_draw(key_list[5], (ABOVE, RHS), 1.0, 6.0, ((0, 256),)),
    }


def product_rows(matrix, right):
    blocks = matrix.reshape(-1, 1024, matrix.shape[1])

    def one_block(rows_block):
        return jnp.dot(rows_block, right, preferred_element_type=jnp.float32)

    return lax.map(one_block, blocks).reshape(matrix.shape[0], right.shape[1])


def reference(inverse, coupling, panel, modes, rhs_window, rhs_above):
    second_block = jnp.dot(inverse[1], rhs_window[1], preferred_element_type=jnp.float32).astype(jnp.bfloat16)
    carried = jnp.dot(coupling, second_block, preferred_element_type=jnp.float32)
    reduced = (rhs_window[0].astype(jnp.float32) - carried).astype(jnp.bfloat16)
    first_block = jnp.dot(inverse[0], reduced, preferred_element_type=jnp.float32).astype(jnp.bfloat16)
    potential = jnp.stack([first_block, second_block])
    if panel.shape[1] % 1024 == 0:
        update_first = product_rows(panel[0], first_block)
        update_second = product_rows(panel[1], second_block)
    else:
        update_first = jnp.dot(panel[0], first_block, preferred_element_type=jnp.float32)
        update_second = jnp.dot(panel[1], second_block, preferred_element_type=jnp.float32)
    above_rows = rhs_above.astype(jnp.float32) - update_first - update_second
    forces = jnp.dot(modes[0], first_block, preferred_element_type=jnp.float32) + jnp.dot(modes[1], second_block, preferred_element_type=jnp.float32)
    return potential, above_rows, forces
```

```python
import functools

import jax
import jax.numpy as jnp
from jax import lax
from jax.experimental import pallas as pl
from jax.experimental.pallas import tpu as pltpu
from jax.sharding import PartitionSpec as P

MESH = pl.DeviceIdType.MESH
CHUNKS = 4
SKEW = 0.0
N_SEMS = 4 * 60 + 16
BF16 = jnp.bfloat16
F32 = jnp.float32


def kernel(
    inv_ref, coup_ref, panel_ref, modes_ref, rhsw_ref, rhsa_ref,
    pot_ref, above_ref, forces_ref,
    g, part, r1, part2, r2, part3, r3, xs, cpart, cr1, cp2, cr2,
    fpart, fr1, fp2, fr2, fo, fot, fob, fob1, fo2, fo2r, fin,
    send_sems, recv_sems,
):
    w = g.shape[-1]
    row = lax.axis_index("prow")
    col = lax.axis_index("pcol")
    h, x, y = row // 16, (row // 4) % 4, row % 4
    zl, k = col // 2, col % 2

    def at_x(d):
        return (h * 16 + ((x + d) % 4) * 4 + y, col)

    def at_y(d):
        return (h * 16 + x * 4 + (y + d) % 4, col)

    def at_z(d):
        return (row, ((zl + d) % 4) * 2 + k)

    at_h = ((1 - h) * 16 + x * 4 + y, col)
    sibling = (row, zl * 2 + 1 - k)

    barrier = pltpu.get_barrier_semaphore()
    partners = [at_x(d) for d in (1, 2, 3)] + [at_y(d) for d in (1, 2, 3)]
    partners += [at_z(d) for d in (1, 2, 3)] + [at_h, sibling]
    for partner in partners:
        pl.semaphore_signal(barrier, inc=1, device_id=partner, device_id_type=MESH)
    pl.semaphore_wait(barrier, len(partners))

    sent = []
    pending = {}

    def send(key, src, dst, device):
        i = len(sent)
        copy = pltpu.make_async_remote_copy(
            src_ref=src, dst_ref=dst, send_sem=send_sems.at[i], recv_sem=recv_sems.at[i],
            device_id=device, device_id_type=MESH,
        )
        copy.start()
        sent.append(copy)
        pending.setdefault(key, []).append(copy)

    def arrived(key):
        for copy in pending.pop(key):
            copy.wait_recv()

    def cols(j):
        return pl.ds(j * w, w)

    def first_axis(j):
        return "y" if j % 2 == 0 else "x"

    def gather_z(b, j):
        for d in (1, 2, 3):
            send(("gz", b, j), g.at[b, j, zl, k], g.at[b, j, zl, k], at_z(d))

    def load_rhs(j):
        g[1, j, zl, k] = rhsw_ref[1, :, cols(j)]
        gather_z(1, j)

    def gather_core(b, j):
        arrived(("gz", b, j))
        send(("gc", b, j), g.at[b, j, :, k], g.at[b, j, :, k], sibling)

    def solve(b, j):
        arrived(("gc", b, j))
        right = g[b, j].reshape(128, w)

        def tile(t, carry):
            rows = inv_ref[b, pl.ds(pl.multiple_of(t * 128, 128), 128), :]
            value = jnp.dot(rows, right, preferred_element_type=F32).astype(BF16)
            part[b, j, t // 2, pl.ds((t % 2) * 2, 2)] = value.reshape(2, 4, 16, w)
            return carry

        lax.fori_loop(0, 4, tile, 0)
        for d in (1, 2, 3):
            if first_axis(j) == "y":
                send(("r1", b, j), part.at[b, j, :, :, (y + d) % 4], r1.at[b, j, d - 1], at_y(d))
            else:
                send(("r1", b, j), part.at[b, j, :, (x + d) % 4], r1.at[b, j, d - 1], at_x(d))

    def reduce_second(b, j):
        arrived(("r1", b, j))
        own = part[b, j, :, :, y] if first_axis(j) == "y" else part[b, j, :, x]
        total = own.astype(F32) + r1[b, j, 0].astype(F32)
        total = total + r1[b, j, 1].astype(F32) + r1[b, j, 2].astype(F32)
        part2[b, j] = total.astype(BF16)
        for d in (1, 2, 3):
            if first_axis(j) == "y":
                send(("r2", b, j), part2.at[b, j, :, (x + d) % 4], r2.at[b, j, d - 1], at_x(d))
            else:
                send(("r2", b, j), part2.at[b, j, :, (y + d) % 4], r2.at[b, j, d - 1], at_y(d))

    def reduce_h(b, j):
        arrived(("r2", b, j))
        own = part2[b, j, :, x] if first_axis(j) == "y" else part2[b, j, :, y]
        total = own.astype(F32) + r2[b, j, 0].astype(F32)
        total = total + r2[b, j, 1].astype(F32) + r2[b, j, 2].astype(F32)
        part3[b, j] = total.astype(BF16)
        send(("r3", b, j), part3.at[b, j], r3.at[b, j], at_h)

    def solved(b, j):
        arrived(("r3", b, j))
        value = (part3[b, j].astype(F32) + r3[b, j].astype(F32)).astype(BF16)
        xs[b, j, :, x, y] = value
        pot_ref[b, :, cols(j)] = xs[b, j, h, x, y]
        block = xs.at[b, j, :, x, y]
        for d in (1, 2, 3):
            send(("g2", b, j), block, block, at_x(d) if first_axis(j) == "y" else at_y(d))

    def gather_first(b, j):
        arrived(("g2", b, j))
        for d in (1, 2, 3):
            if first_axis(j) == "y":
                send(("g1", b, j), xs.at[b, j, :, :, y], xs.at[b, j, :, :, y], at_y(d))
            else:
                send(("g1", b, j), xs.at[b, j, :, x], xs.at[b, j, :, x], at_x(d))

    def couple(j):
        arrived(("g1", 1, j))
        value = jnp.dot(coup_ref[...], xs[1, j].reshape(512, w), preferred_element_type=F32)
        cpart[j] = value.astype(BF16).reshape(4, 2, 16, w)
        send(("c1", j), cpart.at[j, :, 1 - k], cr1.at[j], sibling)

    def couple_z(j):
        arrived(("c1", j))
        cp2[j] = (cpart[j, :, k].astype(F32) + cr1[j].astype(F32)).astype(BF16)
        for d in (1, 2, 3):
            send(("c2", j), cp2.at[j, (zl + d) % 4], cr2.at[j, d - 1], at_z(d))

    def reduced(j):
        arrived(("c2", j))
        carried = cp2[j, zl].astype(F32) + cr2[j, 0].astype(F32)
        carried = carried + cr2[j, 1].astype(F32) + cr2[j, 2].astype(F32)
        g[0, j, zl, k] = (rhsw_ref[0, :, cols(j)].astype(F32) - carried).astype(BF16)
        gather_z(0, j)

    def above(j):
        arrived(("g1", 0, j))

        def tile(t, carry):
            rows = pl.ds(pl.multiple_of(t * 192, 192), 192)
            value = jnp.dot(panel_ref[0, rows, :], xs[0, j].reshape(512, w), preferred_element_type=F32)
            value += jnp.dot(panel_ref[1, rows, :], xs[1, j].reshape(512, w), preferred_element_type=F32)
            fpart[j, t // 2, t % 2] = value.astype(BF16)
            return carry

        lax.fori_loop(0, 8, tile, 0)
        send(("f1", j), fpart.at[j, :, 1 - k], fr1.at[j], sibling)
        value = jnp.dot(modes_ref[0], xs[0, j].reshape(512, w), preferred_element_type=F32)
        value += jnp.dot(modes_ref[1], xs[1, j].reshape(512, w), preferred_element_type=F32)
        fo[:, cols(j)] = value

    def above_z(j):
        arrived(("f1", j))

        def tile(t, carry):
            fp2[j, t] = (fpart[j, t, k].astype(F32) + fr1[j, t].astype(F32)).astype(BF16)
            return carry

        lax.fori_loop(0, 4, tile, 0)
        for d in (2, 1, 3):
            send(("f2", j), fp2.at[j, (zl + d) % 4], fr2.at[j, d - 1], at_z(d))

    def above_end(j):
        arrived(("f2", j))
        total = fp2[j, zl].astype(F32) + fr2[j, 0].astype(F32)
        total = total + fr2[j, 1].astype(F32) + fr2[j, 2].astype(F32)
        above_ref[:, cols(j)] = rhsa_ref[:, cols(j)].astype(F32) - total

    def forces_core():
        for m in range(16):
            for n in range(8):
                fot[pl.ds(m * 8 + n, 1), :] = fo[pl.ds(m, 1), pl.ds(n * 128, 128)]
        fob[...] = fot[...].astype(BF16).reshape(4, 2, 16, 128)
        send("o1", fob.at[:, 1 - k], fob1, sibling)

    def forces_z():
        arrived("o1")
        fo2[...] = (fob[:, k].astype(F32) + fob1[...].astype(F32)).astype(BF16)
        for d in (1, 2, 3):
            send("o2", fo2.at[(zl + d) % 4], fo2r.at[d - 1], at_z(d))

    def forces_end():
        arrived("o2")
        total = fo2[zl].astype(F32) + fo2r[0].astype(F32)
        fin[...] = total + fo2r[1].astype(F32) + fo2r[2].astype(F32)
        for m in range(2):
            for n in range(8):
                forces_ref[pl.ds(m, 1), pl.ds(n * 128, 128)] = fin[pl.ds(m * 8 + n, 1), :]

    last = CHUNKS - 1
    plan = []
    for j in range(CHUNKS):
        steps = [functools.partial(load_rhs, j)]
        for b in (1, 0):
            for step in (gather_core, solve, reduce_second, reduce_h, solved, gather_first):
                steps.append(functools.partial(step, b, j))
            if b == 1:
                steps += [functools.partial(step, j) for step in (couple, couple_z, reduced)]
        steps.append(functools.partial(above, j))
        for s, step in enumerate(steps):
            plan.append((s + SKEW * j, j, step))
        base = len(steps)
        plan.append((base + SKEW * j, j, functools.partial(above_z, j)))
        plan.append((base + 1 + SKEW * j, j, functools.partial(above_end, j)))
        if j == last:
            plan.append((base - 0.5 + SKEW * j, j, forces_core))
            plan.append((base + 0.5 + SKEW * j, j, forces_z))
            plan.append((base + 1.5 + SKEW * j, j, forces_end))
    for _, _, step in sorted(plan, key=lambda item: (item[0], item[1])):
        step()
    for copy in sent:
        copy.wait_send()


def body(inverse, coupling, panel, modes, rhs_window, rhs_above):
    n, w = CHUNKS, 1024 // CHUNKS
    vmem = pl.BlockSpec(memory_space=pltpu.VMEM)

    def buf(*shape):
        return pltpu.VMEM(shape, BF16)

    return tuple(pl.pallas_call(
        kernel,
        out_shape=(
            jax.ShapeDtypeStruct((2, 16, 1024), BF16),
            jax.ShapeDtypeStruct((192, 1024), F32),
            jax.ShapeDtypeStruct((2, 1024), F32),
        ),
        in_specs=[vmem] * 6,
        out_specs=(vmem,) * 3,
        scratch_shapes=[
            buf(2, n, 4, 2, 16, w),
            buf(2, n, 2, 4, 4, 16, w),
            buf(2, n, 3, 2, 4, 16, w),
            buf(2, n, 2, 4, 16, w),
            buf(2, n, 3, 2, 16, w),
            buf(2, n, 2, 16, w),
            buf(2, n, 2, 16, w),
            buf(2, n, 2, 4, 4, 16, w),
            buf(n, 4, 2, 16, w),
            buf(n, 4, 16, w),
            buf(n, 4, 16, w),
            buf(n, 3, 16, w),
            buf(n, 4, 2, 192, w),
            buf(n, 4, 192, w),
            buf(n, 4, 192, w),
            buf(n, 3, 192, w),
            pltpu.VMEM((16, 1024), F32),
            pltpu.VMEM((128, 128), F32),
            buf(4, 2, 16, 128),
            buf(4, 16, 128),
            buf(4, 16, 128),
            buf(3, 16, 128),
            pltpu.VMEM((16, 128), F32),
            pltpu.SemaphoreType.DMA((N_SEMS,)),
            pltpu.SemaphoreType.DMA((N_SEMS,)),
        ],
        compiler_params=pltpu.CompilerParams(
            collective_id=0, has_side_effects=True, vmem_limit_bytes=48 * 2**20
        ),
        cost_estimate=pl.CostEstimate(
            flops=3_700_000_000, bytes_accessed=6_000_000, transcendentals=0
        ),
    )(inverse, coupling, panel, modes, rhs_window, rhs_above))


def solution(mesh):
    placed = (
        P(None, "pcol", "prow"),
        P("prow", "pcol"),
        P(None, "prow", "pcol"),
        P(None, "prow", "pcol"),
        P(None, ("prow", "pcol"), None),
        P(("prow", "pcol"), None),
    )
    return jax.shard_map(
        body,
        mesh=mesh,
        in_specs=placed,
        out_specs=(
            P(None, ("pcol", "prow"), None),
            P(("prow", "pcol"), None),
            P(("prow", "pcol"), None),
        ),
        check_vma=False,
    )
```

```python
import functools

import jax
import jax.numpy as jnp
from jax import lax
from jax.experimental import pallas as pl
from jax.experimental.pallas import tpu as pltpu
from jax.sharding import PartitionSpec as P

MESH = pl.DeviceIdType.MESH
CHUNKS = 4
SKEW = 0.0
GROUP = 4
TAIL = 0.1
LATE = 0.0
N_SEMS = 4 * 60 + 16
BF16 = jnp.bfloat16
F32 = jnp.float32


def kernel(
    inv_hbm, coup_hbm, panel_hbm, modes_hbm, rhsw_hbm, rhsa_hbm,
    pot_ref, above_ref, forces_ref,
    g, part, r1, part2, r2, part3, r3, xs, cpart, cr1, cp2, cr2,
    fpart, fr1, fp2, fr2, fo, fot, fob, fob1, fo2, fo2r, fin,
    inv_ref, coup_ref, panel_ref, modes_ref, rhsw_ref, rhsa_ref,
    load_sems, send_sems, recv_sems, fm, f2_send, f2_recv,
):
    w = g.shape[-1]
    loads = {}
    for name, src, dst in (
        ("rhsw", rhsw_hbm, rhsw_ref),
        ("inv", inv_hbm, inv_ref),
        ("coup", coup_hbm, coup_ref),
        ("panel", panel_hbm, panel_ref),
        ("modes", modes_hbm, modes_ref),
        ("rhsa", rhsa_hbm, rhsa_ref),
    ):
        loads[name] = pltpu.make_async_copy(src, dst, load_sems.at[len(loads)])
        loads[name].start()

    def loaded(*names):
        for name in names:
            if name in loads:
                loads.pop(name).wait()

    row = lax.axis_index("prow")
    col = lax.axis_index("pcol")
    h, x, y = row // 16, (row // 4) % 4, row % 4
    zl, k = col // 2, col % 2

    def at_x(d):
        return (h * 16 + ((x + d) % 4) * 4 + y, col)

    def at_y(d):
        return (h * 16 + x * 4 + (y + d) % 4, col)

    def at_z(d):
        return (row, ((zl + d) % 4) * 2 + k)

    outer = jnp.logical_or(zl == 0, zl == 3)
    near = jnp.where(zl < 2, 1 - zl, 5 - zl)
    far = 3 - near

    at_h = ((1 - h) * 16 + x * 4 + y, col)
    sibling = (row, zl * 2 + 1 - k)

    barrier = pltpu.get_barrier_semaphore()
    partners = [at_x(d) for d in (1, 2, 3)] + [at_y(d) for d in (1, 2, 3)]
    partners += [at_z(d) for d in (1, 2, 3)] + [at_h, sibling]
    for partner in partners:
        pl.semaphore_signal(barrier, inc=1, device_id=partner, device_id_type=MESH)
    pl.semaphore_wait(barrier, len(partners))

    sent = []
    pending = {}

    def send(key, src, dst, device):
        i = len(sent)
        copy = pltpu.make_async_remote_copy(
            src_ref=src, dst_ref=dst, send_sem=send_sems.at[i], recv_sem=recv_sems.at[i],
            device_id=device, device_id_type=MESH,
        )
        copy.start()
        sent.append(copy)
        pending.setdefault(key, []).append(copy)

    def arrived(key):
        for copy in pending.pop(key):
            copy.wait_recv()

    def cols(j):
        return pl.ds(j * w, w)

    def first_axis(j):
        return "y" if j % 2 == 0 else "x"

    def gather_z(b, j):
        for d in (1, 2, 3):
            send(("gz", b, j), g.at[b, j, zl, k], g.at[b, j, zl, k], at_z(d))

    def load_rhs(j):
        loaded("rhsw")
        g[1, j, zl, k] = rhsw_ref[1, :, cols(j)]
        gather_z(1, j)

    def gather_core(b, j):
        arrived(("gz", b, j))
        send(("gc", b, j), g.at[b, j, :, k], g.at[b, j, :, k], sibling)

    def solve(b, j):
        loaded("inv")
        arrived(("gc", b, j))
        right = g[b, j].reshape(128, w)

        def tile(t, carry):
            rows = inv_ref[b, pl.ds(pl.multiple_of(t * 128, 128), 128), :]
            value = jnp.dot(rows, right, preferred_element_type=F32).astype(BF16)
            part[b, j, t // 2, pl.ds((t % 2) * 2, 2)] = value.reshape(2, 4, 16, w)
            return carry

        lax.fori_loop(0, 4, tile, 0)
        for d in (1, 2, 3):
            if first_axis(j) == "y":
                send(("r1", b, j), part.at[b, j, :, :, (y + d) % 4], r1.at[b, j, d - 1], at_y(d))
            else:
                send(("r1", b, j), part.at[b, j, :, (x + d) % 4], r1.at[b, j, d - 1], at_x(d))

    def reduce_second(b, j):
        arrived(("r1", b, j))
        own = part[b, j, :, :, y] if first_axis(j) == "y" else part[b, j, :, x]
        total = own.astype(F32) + r1[b, j, 0].astype(F32)
        total = total + r1[b, j, 1].astype(F32) + r1[b, j, 2].astype(F32)
        part2[b, j] = total.astype(BF16)
        for d in (1, 2, 3):
            if first_axis(j) == "y":
                send(("r2", b, j), part2.at[b, j, :, (x + d) % 4], r2.at[b, j, d - 1], at_x(d))
            else:
                send(("r2", b, j), part2.at[b, j, :, (y + d) % 4], r2.at[b, j, d - 1], at_y(d))

    def reduce_h(b, j):
        arrived(("r2", b, j))
        own = part2[b, j, :, x] if first_axis(j) == "y" else part2[b, j, :, y]
        total = own.astype(F32) + r2[b, j, 0].astype(F32)
        total = total + r2[b, j, 1].astype(F32) + r2[b, j, 2].astype(F32)
        part3[b, j] = total.astype(BF16)
        send(("r3", b, j), part3.at[b, j], r3.at[b, j], at_h)

    def solved(b, j):
        arrived(("r3", b, j))
        value = (part3[b, j].astype(F32) + r3[b, j].astype(F32)).astype(BF16)
        xs[b, j, :, x, y] = value
        pot_ref[b, :, cols(j)] = xs[b, j, h, x, y]
        block = xs.at[b, j, :, x, y]
        for d in (1, 2, 3):
            send(("g2", b, j), block, block, at_x(d) if first_axis(j) == "y" else at_y(d))

    def gather_first(b, j):
        arrived(("g2", b, j))
        for d in (1, 2, 3):
            if first_axis(j) == "y":
                send(("g1", b, j), xs.at[b, j, :, :, y], xs.at[b, j, :, :, y], at_y(d))
            else:
                send(("g1", b, j), xs.at[b, j, :, x], xs.at[b, j, :, x], at_x(d))

    def couple(j):
        loaded("coup")
        arrived(("g1", 1, j))
        value = jnp.dot(coup_ref[...], xs[1, j].reshape(512, w), preferred_element_type=F32)
        cpart[j] = value.astype(BF16).reshape(4, 2, 16, w)
        send(("c1", j), cpart.at[j, :, 1 - k], cr1.at[j], sibling)

    def couple_z(j):
        arrived(("c1", j))
        cp2[j] = (cpart[j, :, k].astype(F32) + cr1[j].astype(F32)).astype(BF16)
        for d in (1, 2, 3):
            send(("c2", j), cp2.at[j, (zl + d) % 4], cr2.at[j, d - 1], at_z(d))

    def reduced(j):
        arrived(("c2", j))
        carried = cp2[j, zl].astype(F32) + cr2[j, 0].astype(F32)
        carried = carried + cr2[j, 1].astype(F32) + cr2[j, 2].astype(F32)
        g[0, j, zl, k] = (rhsw_ref[0, :, cols(j)].astype(F32) - carried).astype(BF16)
        gather_z(0, j)

    def above(j):
        loaded("panel", "modes")
        arrived(("g1", 0, j))

        def tile(t, carry):
            rows = pl.ds(pl.multiple_of(t * 192, 192), 192)
            value = jnp.dot(panel_ref[0, rows, :], xs[0, j].reshape(512, w), preferred_element_type=F32)
            value += jnp.dot(panel_ref[1, rows, :], xs[1, j].reshape(512, w), preferred_element_type=F32)
            fpart[j, t // 2, t % 2] = value.astype(BF16)
            return carry

        lax.fori_loop(0, 8, tile, 0)
        send(("f1", j), fpart.at[j, :, 1 - k], fr1.at[j], sibling)
        value = jnp.dot(modes_ref[0], xs[0, j].reshape(512, w), preferred_element_type=F32)
        value += jnp.dot(modes_ref[1], xs[1, j].reshape(512, w), preferred_element_type=F32)
        fo[:, cols(j)] = value

    def above_z(j):
        arrived(("f1", j))

        def tile(t, carry):
            fp2[j, t] = (fpart[j, t, k].astype(F32) + fr1[j, t].astype(F32)).astype(BF16)
            return carry

        lax.fori_loop(0, 4, tile, 0)
        @pl.when(outer)
        def _():
            f2_copy(j, 0, fp2.at[j, 3 - zl], fm.at[j], 3, near).start()
            f2_copy(j, 1, fp2.at[j, far], fr2.at[j, 2], 2, far).start()
            f2_copy(j, 2, fp2.at[j, near], fr2.at[j, 1], 1, near).start()
            fr2[j, 2] = jnp.zeros_like(fr2[j, 2])

        @pl.when(jnp.logical_not(outer))
        def _():
            f2_copy(j, 0, fp2.at[j, 3 - zl], fr2.at[j, 0], 0, 3 - zl).start()
            f2_copy(j, 1, fp2.at[j, near], fr2.at[j, 0], 0, near).start()

    def f2_copy(j, slot, src, dst, landing, line):
        return pltpu.make_async_remote_copy(
            src_ref=src, dst_ref=dst, send_sem=f2_send.at[j, slot], recv_sem=f2_recv.at[j, landing],
            device_id=(row, line * 2 + k), device_id_type=MESH,
        )

    def above_merge(j):
        @pl.when(jnp.logical_not(outer))
        def _():
            f2_copy(j, 0, fp2.at[j, far], fm.at[j], 3, far).wait_recv()
            merged = fp2[j, far].astype(F32) + fm[j].astype(F32)
            fp2[j, far] = merged.astype(BF16)
            f2_copy(j, 2, fp2.at[j, far], fr2.at[j, 1], 1, far).start()

    def above_end(j):
        loaded("rhsa")
        f2_copy(j, 0, fp2.at[j, zl], fr2.at[j, 0], 0, near).wait_recv()
        f2_copy(j, 0, fp2.at[j, zl], fr2.at[j, 1], 1, near).wait_recv()

        @pl.when(jnp.logical_not(outer))
        def _():
            f2_copy(j, 0, fp2.at[j, zl], fr2.at[j, 2], 2, near).wait_recv()

        total = fp2[j, zl].astype(F32) + fr2[j, 0].astype(F32)
        total = total + fr2[j, 1].astype(F32) + fr2[j, 2].astype(F32)
        above_ref[:, cols(j)] = rhsa_ref[:, cols(j)].astype(F32) - total
        for slot in range(3):
            f2_copy(j, slot, fp2.at[j, zl], fr2.at[j, 0], 0, near).wait_send()

    def forces_core():
        for m in range(16):
            for n in range(8):
                fot[pl.ds(m * 8 + n, 1), :] = fo[pl.ds(m, 1), pl.ds(n * 128, 128)]
        fob[...] = fot[...].astype(BF16).reshape(4, 2, 16, 128)
        send("o1", fob.at[:, 1 - k], fob1, sibling)

    def forces_z():
        arrived("o1")
        fo2[...] = (fob[:, k].astype(F32) + fob1[...].astype(F32)).astype(BF16)
        for d in (1, 2, 3):
            send("o2", fo2.at[(zl + d) % 4], fo2r.at[d - 1], at_z(d))

    def forces_end():
        arrived("o2")
        total = fo2[zl].astype(F32) + fo2r[0].astype(F32)
        fin[...] = total + fo2r[1].astype(F32) + fo2r[2].astype(F32)
        for m in range(2):
            for n in range(8):
                forces_ref[pl.ds(m, 1), pl.ds(n * 128, 128)] = fin[pl.ds(m * 8 + n, 1), :]

    last = CHUNKS - 1

    def lag(j):
        return SKEW * (j // GROUP)

    plan = []
    for j in range(CHUNKS):
        steps = [functools.partial(load_rhs, j)]
        for b in (1, 0):
            for step in (gather_core, solve, reduce_second, reduce_h, solved, gather_first):
                steps.append(functools.partial(step, b, j))
            if b == 1:
                steps += [functools.partial(step, j) for step in (couple, couple_z, reduced)]
        steps.append(functools.partial(above, j))
        for s, step in enumerate(steps):
            s += TAIL * (j % GROUP) * (s == len(steps) - 1)
            plan.append((s + lag(j), j, step))
        base = len(steps)
        early = LATE * (j // GROUP < last // GROUP)
        start = base - 1 + TAIL * (j % GROUP + 1.5) + lag(j) + early
        plan.append((start, j, functools.partial(above_z, j)))
        plan.append((start + TAIL * 1.2, j, functools.partial(above_merge, j)))
        plan.append((base + 1 + lag(j), j, functools.partial(above_end, j)))
        if j == last:
            plan.append((base - 1 + TAIL * GROUP + lag(j), j, forces_core))
            plan.append((base + 0.5 + lag(j), j, forces_z))
            plan.append((base + 1.5 + lag(j), j, forces_end))
    for _, _, step in sorted(plan, key=lambda item: (item[0], item[1])):
        step()
    for copy in sent:
        copy.wait_send()


def body(inverse, coupling, panel, modes, rhs_window, rhs_above):
    n, w = CHUNKS, 1024 // CHUNKS
    vmem = pl.BlockSpec(memory_space=pltpu.VMEM)

    def buf(*shape):
        return pltpu.VMEM(shape, BF16)

    return tuple(pl.pallas_call(
        kernel,
        out_shape=(
            jax.ShapeDtypeStruct((2, 16, 1024), BF16),
            jax.ShapeDtypeStruct((192, 1024), F32),
            jax.ShapeDtypeStruct((2, 1024), F32),
        ),
        in_specs=[pl.BlockSpec(memory_space=pl.ANY)] * 6,
        out_specs=(vmem,) * 3,
        scratch_shapes=[
            buf(2, n, 4, 2, 16, w),
            buf(2, n, 2, 4, 4, 16, w),
            buf(2, n, 3, 2, 4, 16, w),
            buf(2, n, 2, 4, 16, w),
            buf(2, n, 3, 2, 16, w),
            buf(2, n, 2, 16, w),
            buf(2, n, 2, 16, w),
            buf(2, n, 2, 4, 4, 16, w),
            buf(n, 4, 2, 16, w),
            buf(n, 4, 16, w),
            buf(n, 4, 16, w),
            buf(n, 3, 16, w),
            buf(n, 4, 2, 192, w),
            buf(n, 4, 192, w),
            buf(n, 4, 192, w),
            buf(n, 3, 192, w),
            pltpu.VMEM((16, 1024), F32),
            pltpu.VMEM((128, 128), F32),
            buf(4, 2, 16, 128),
            buf(4, 16, 128),
            buf(4, 16, 128),
            buf(3, 16, 128),
            pltpu.VMEM((16, 128), F32),
            buf(2, 512, 128),
            buf(128, 512),
            buf(2, 1536, 512),
            buf(2, 16, 512),
            buf(2, 16, 1024),
            buf(192, 1024),
            pltpu.SemaphoreType.DMA((6,)),
            pltpu.SemaphoreType.DMA((N_SEMS,)),
            pltpu.SemaphoreType.DMA((N_SEMS,)),
            buf(n, 192, w),
            pltpu.SemaphoreType.DMA((n, 3)),
            pltpu.SemaphoreType.DMA((n, 4)),
        ],
        compiler_params=pltpu.CompilerParams(
            collective_id=0, has_side_effects=True, vmem_limit_bytes=60 * 2**20
        ),
        cost_estimate=pl.CostEstimate(
            flops=3_700_000_000, bytes_accessed=6_000_000, transcendentals=0
        ),
    )(inverse, coupling, panel, modes, rhs_window, rhs_above))


def solution(mesh):
    placed = (
        P(None, "pcol", "prow"),
        P("prow", "pcol"),
        P(None, "prow", "pcol"),
        P(None, "prow", "pcol"),
        P(None, ("prow", "pcol"), None),
        P(("prow", "pcol"), None),
    )
    return jax.shard_map(
        body,
        mesh=mesh,
        in_specs=placed,
        out_specs=(
            P(None, ("pcol", "prow"), None),
            P(("prow", "pcol"), None),
            P(("prow", "pcol"), None),
        ),
        check_vma=False,
    )
```

```python
import functools

import jax
import jax.numpy as jnp
from jax import lax
from jax.experimental import pallas as pl
from jax.experimental.pallas import tpu as pltpu
from jax.sharding import PartitionSpec as P

MESH = pl.DeviceIdType.MESH
CHUNKS = 2
HALF = 512
TAIL = 0.8
N_SEMS = 200
BF16 = jnp.bfloat16
F32 = jnp.float32


def kernel(
    inv_hbm, coup_hbm, panel_hbm, modes_hbm, rhsw_hbm, rhsa_hbm,
    pot_ref, above_ref, forces_ref,
    g, part, r1, part2, r2, xs, cpart, cr1, cp2, cr2,
    fpart, fr1, fp2, fr2, fo, fot, fob, fob1, fo2, fo2r, fin,
    inv2, coup2, panel_ref, modes_ref, rhsw_ref, rhsa_ref, rw0,
    load_sems, send_sems, recv_sems, fm, f2_send, f2_recv,
):
    w = g.shape[-1]
    row = lax.axis_index("prow")
    col = lax.axis_index("pcol")
    h, x, y = row // 16, (row // 4) % 4, row % 4
    zl, k = col // 2, col % 2

    loads = {}
    for name, src, dst in (
        ("rhsw", rhsw_hbm, rhsw_ref),
        ("inv1", inv_hbm.at[1], inv2.at[1, h]),
        ("coup", coup_hbm, coup2.at[h]),
        ("inv0", inv_hbm.at[0], inv2.at[0, h]),
        ("panel", panel_hbm, panel_ref),
        ("modes", modes_hbm, modes_ref),
        ("rhsa", rhsa_hbm, rhsa_ref),
    ):
        loads[name] = pltpu.make_async_copy(src, dst, load_sems.at[len(loads)])
        loads[name].start()

    def loaded(*names):
        for name in names:
            if name in loads:
                loads.pop(name).wait()

    def at_x(d):
        return (h * 16 + ((x + d) % 4) * 4 + y, col)

    def at_y(d):
        return (h * 16 + x * 4 + (y + d) % 4, col)

    def at_z(d):
        return (row, ((zl + d) % 4) * 2 + k)

    outer = jnp.logical_or(zl == 0, zl == 3)
    near = jnp.where(zl < 2, 1 - zl, 5 - zl)
    far = 3 - near

    def across_h(d):
        return ((1 - h) * 16 + x * 4 + y, ((zl + d) % 4) * 2 + k)

    at_h = ((1 - h) * 16 + x * 4 + y, col)
    sibling = (row, zl * 2 + 1 - k)

    barrier = pltpu.get_barrier_semaphore()
    partners = [at_x(d) for d in (1, 2, 3)] + [at_y(d) for d in (1, 2, 3)]
    partners += [at_z(d) for d in (1, 2, 3)] + [at_h, sibling]
    partners += [across_h(d) for d in (1, 2, 3)]
    for partner in partners:
        pl.semaphore_signal(barrier, inc=1, device_id=partner, device_id_type=MESH)
    pl.semaphore_wait(barrier, len(partners))

    sent = []
    pending = {}

    def send(key, src, dst, device):
        i = len(sent)
        copy = pltpu.make_async_remote_copy(
            src_ref=src, dst_ref=dst, send_sem=send_sems.at[i], recv_sem=recv_sems.at[i],
            device_id=device, device_id_type=MESH,
        )
        copy.start()
        sent.append(copy)
        pending.setdefault(key, []).append(copy)

    def arrived(key):
        for copy in pending.pop(key, ()):
            copy.wait_recv()

    def cols(half, j):
        return pl.ds(pl.multiple_of(half * HALF + j * w, 128), w)

    def first_axis(j):
        return "y" if j % 2 == 0 else "x"

    def load_rhs(j):
        loaded("rhsw")
        g[1, j, h, zl, k] = rhsw_ref[1, :, cols(h, j)]
        mine = g.at[1, j, h, zl, k]
        for d in (1, 2, 3):
            send(("gz", 1, j), mine, mine, at_z(d))
        for d in range(4):
            send(("gz", 1, j), rhsw_ref.at[1, :, cols(1 - h, j)], mine, across_h(d))

    def swap_inverse():
        send("inv1", inv_hbm.at[1], inv2.at[1, h], at_h)

    def swap_rhs():
        send("rw0", rhsw_ref.at[0, :, pl.ds(pl.multiple_of((1 - h) * HALF, 128), HALF)], rw0, at_h)

    def swap_coupling(part_no):
        rows = pl.ds(part_no * 32, 32)
        send("coup", coup_hbm.at[rows], coup2.at[h, rows], at_h)

    def swap_first(part_no):
        rows = pl.ds(part_no * 128, 128)
        send("inv0", inv_hbm.at[0, rows], inv2.at[0, h, rows], at_h)

    def gather_z(j):
        for d in (1, 2, 3):
            send(("gz", 0, j), g.at[0, j, :, zl, k], g.at[0, j, :, zl, k], at_z(d))

    def gather_core(b, j):
        arrived(("gz", b, j))
        send(("gc", b, j), g.at[b, j, :, :, k], g.at[b, j, :, :, k], sibling)

    def solve(b, j):
        loaded("inv%d" % b)
        arrived("inv%d" % b)
        arrived(("gc", b, j))
        right = g[b, j].reshape(2, 128, w)

        def tile(t, carry):
            rows = pl.ds(pl.multiple_of(t * 128, 128), 128)
            value = jnp.dot(inv2[b, 0, rows, :], right[0], preferred_element_type=F32)
            value += jnp.dot(inv2[b, 1, rows, :], right[1], preferred_element_type=F32)
            part[b, j, t // 2, pl.ds((t % 2) * 2, 2)] = value.astype(BF16).reshape(2, 4, 16, w)
            return carry

        lax.fori_loop(0, 4, tile, 0)
        for d in (1, 2, 3):
            if first_axis(j) == "y":
                send(("r1", b, j), part.at[b, j, :, :, (y + d) % 4], r1.at[b, j, d - 1], at_y(d))
            else:
                send(("r1", b, j), part.at[b, j, :, (x + d) % 4], r1.at[b, j, d - 1], at_x(d))

    def reduce_second(b, j):
        arrived(("r1", b, j))
        own = part[b, j, :, :, y] if first_axis(j) == "y" else part[b, j, :, x]
        total = own.astype(F32) + r1[b, j, 0].astype(F32)
        total = total + r1[b, j, 1].astype(F32) + r1[b, j, 2].astype(F32)
        part2[b, j] = total.astype(BF16)
        for d in (1, 2, 3):
            if first_axis(j) == "y":
                send(("r2", b, j), part2.at[b, j, :, (x + d) % 4], r2.at[b, j, d - 1], at_x(d))
            else:
                send(("r2", b, j), part2.at[b, j, :, (y + d) % 4], r2.at[b, j, d - 1], at_y(d))

    def spread_second(b, half, q, j):
        block = xs.at[b, half, j, :, x, y]
        for d in (1, 2, 3):
            send(("g2", b, q, j), block, block, at_x(d) if first_axis(j) == "y" else at_y(d))

    def solved(b, j):
        arrived(("r2", b, j))
        own = part2[b, j, :, x] if first_axis(j) == "y" else part2[b, j, :, y]
        total = own.astype(F32) + r2[b, j, 0].astype(F32)
        total = total + r2[b, j, 1].astype(F32) + r2[b, j, 2].astype(F32)
        xs[b, h, j, :, x, y] = total.astype(BF16)
        block = xs.at[b, h, j, :, x, y]
        if b == 0:
            send(("hh", b, j), block, block, at_h)
        spread_second(b, h, 0, j)
        if b == 1:
            send(("hh", b, j), block, block, at_h)
        pot_ref[b, :, cols(h, j)] = xs[b, h, j, h, x, y]

    def other_solved(b, j):
        arrived(("hh", b, j))
        spread_second(b, 1 - h, 1, j)
        pot_ref[b, :, cols(1 - h, j)] = xs[b, 1 - h, j, h, x, y]

    def gather_first(b, q, j):
        arrived(("g2", b, q, j))
        half = h if q == 0 else 1 - h
        for d in (1, 2, 3):
            if first_axis(j) == "y":
                block = xs.at[b, half, j, :, :, y]
                send(("g1", b, q, j), block, block, at_y(d))
            else:
                block = xs.at[b, half, j, :, x]
                send(("g1", b, q, j), block, block, at_x(d))

    def couple(j):
        loaded("coup")
        arrived("coup")
        arrived(("g1", 1, 0, j))
        right = xs[1, h, j].reshape(512, w)
        for side in range(2):
            value = jnp.dot(coup2[side], right, preferred_element_type=F32)
            cpart[j, side] = value.astype(BF16).reshape(4, 2, 16, w)
        send(("c1", j), cpart.at[j, :, :, 1 - k], cr1.at[j], sibling)

    def couple_z(j):
        arrived(("c1", j))
        cp2[j] = (cpart[j, :, :, k].astype(F32) + cr1[j].astype(F32)).astype(BF16)
        for d in (1, 2, 3):
            send(("c2", j), cp2.at[j, :, (zl + d) % 4], cr2.at[j, d - 1], at_z(d))

    def reduced(j):
        arrived(("c2", j))
        arrived("rw0")
        for side, rhs in ((h, rhsw_ref[0, :, cols(h, j)]), (1 - h, rw0[:, pl.ds(j * w, w)])):
            carried = cp2[j, side, zl].astype(F32) + cr2[j, 0, side].astype(F32)
            carried = carried + cr2[j, 1, side].astype(F32) + cr2[j, 2, side].astype(F32)
            g[0, j, side, zl, k] = (rhs.astype(F32) - carried).astype(BF16)
        gather_z(j)

    def above(q, i):
        j = q * CHUNKS + i
        half = h if q == 0 else 1 - h
        loaded("panel", "modes")
        arrived(("g1", 1, q, i))
        arrived(("g1", 0, q, i))

        def tile(t, carry):
            rows = pl.ds(pl.multiple_of(t * 192, 192), 192)
            value = jnp.dot(panel_ref[0, rows, :], xs[0, half, i].reshape(512, w), preferred_element_type=F32)
            value += jnp.dot(panel_ref[1, rows, :], xs[1, half, i].reshape(512, w), preferred_element_type=F32)
            fpart[j, t // 2, t % 2] = value.astype(BF16)
            return carry

        lax.fori_loop(0, 8, tile, 0)
        send(("f1", j), fpart.at[j, :, 1 - k], fr1.at[j], sibling)
        value = jnp.dot(modes_ref[0], xs[0, half, i].reshape(512, w), preferred_element_type=F32)
        value += jnp.dot(modes_ref[1], xs[1, half, i].reshape(512, w), preferred_element_type=F32)
        fo[:, cols(half, i)] = value

    def above_z(j):
        arrived(("f1", j))

        def tile(t, carry):
            fp2[j, t] = (fpart[j, t, k].astype(F32) + fr1[j, t].astype(F32)).astype(BF16)
            return carry

        lax.fori_loop(0, 4, tile, 0)
        @pl.when(outer)
        def _():
            f2_copy(j, 0, fp2.at[j, 3 - zl], fm.at[j], 3, near).start()
            f2_copy(j, 1, fp2.at[j, far], fr2.at[j, 2], 2, far).start()
            f2_copy(j, 2, fp2.at[j, near], fr2.at[j, 1], 1, near).start()
            fr2[j, 2] = jnp.zeros_like(fr2[j, 2])

        @pl.when(jnp.logical_not(outer))
        def _():
            f2_copy(j, 0, fp2.at[j, 3 - zl], fr2.at[j, 0], 0, 3 - zl).start()
            f2_copy(j, 1, fp2.at[j, near], fr2.at[j, 0], 0, near).start()

    def f2_copy(j, slot, src, dst, landing, line):
        return pltpu.make_async_remote_copy(
            src_ref=src, dst_ref=dst, send_sem=f2_send.at[j, slot], recv_sem=f2_recv.at[j, landing],
            device_id=(row, line * 2 + k), device_id_type=MESH,
        )

    def above_merge(j):
        @pl.when(jnp.logical_not(outer))
        def _():
            f2_copy(j, 0, fp2.at[j, far], fm.at[j], 3, far).wait_recv()
            merged = fp2[j, far].astype(F32) + fm[j].astype(F32)
            fp2[j, far] = merged.astype(BF16)
            f2_copy(j, 2, fp2.at[j, far], fr2.at[j, 1], 1, far).start()

    def above_end(j):
        loaded("rhsa")
        f2_copy(j, 0, fp2.at[j, zl], fr2.at[j, 0], 0, near).wait_recv()
        f2_copy(j, 0, fp2.at[j, zl], fr2.at[j, 1], 1, near).wait_recv()

        @pl.when(jnp.logical_not(outer))
        def _():
            f2_copy(j, 0, fp2.at[j, zl], fr2.at[j, 2], 2, near).wait_recv()

        total = fp2[j, zl].astype(F32) + fr2[j, 0].astype(F32)
        total = total + fr2[j, 1].astype(F32) + fr2[j, 2].astype(F32)
        here = cols(h if j < CHUNKS else 1 - h, j % CHUNKS)
        above_ref[:, here] = rhsa_ref[:, here].astype(F32) - total
        for slot in range(3):
            f2_copy(j, slot, fp2.at[j, zl], fr2.at[j, 0], 0, near).wait_send()

    def forces_core():
        for m in range(16):
            for n in range(8):
                fot[pl.ds(m * 8 + n, 1), :] = fo[pl.ds(m, 1), pl.ds(n * 128, 128)]
        fob[...] = fot[...].astype(BF16).reshape(4, 2, 16, 128)
        send("o1", fob.at[:, 1 - k], fob1, sibling)

    def forces_z():
        arrived("o1")
        fo2[...] = (fob[:, k].astype(F32) + fob1[...].astype(F32)).astype(BF16)
        for d in (1, 2, 3):
            send("o2", fo2.at[(zl + d) % 4], fo2r.at[d - 1], at_z(d))

    def forces_end():
        arrived("o2")
        total = fo2[zl].astype(F32) + fo2r[0].astype(F32)
        fin[...] = total + fo2r[1].astype(F32) + fo2r[2].astype(F32)
        for m in range(2):
            for n in range(8):
                forces_ref[pl.ds(m, 1), pl.ds(n * 128, 128)] = fin[pl.ds(m * 8 + n, 1), :]

    plan = []

    def at(place, step, *args):
        plan.append((place, len(plan), functools.partial(step, *args)))

    for j in range(CHUNKS):
        late = 0.1 * j
        at(0.0 + late, load_rhs, j)
        at(1.0 + late, gather_core, 1, j)
        at(2.0 + late, solve, 1, j)
        at(3.0 + late, reduce_second, 1, j)
        at(4.0 + late, solved, 1, j)
        at(5.0 + late, gather_first, 1, 0, j)
        at(6.0 + late, couple, j)
        at(6.5 + late, other_solved, 1, j)
        at(7.0 + late, couple_z, j)
        at(7.5 + late, gather_first, 1, 1, j)
        at(8.0 + late, reduced, j)
        at(9.0 + late, gather_core, 0, j)
        at(10.0 + late, solve, 0, j)
        at(11.0 + late, reduce_second, 0, j)
        at(12.0 + late, solved, 0, j)
        at(13.0 + late, gather_first, 0, 0, j)
        at(13.5 + late, other_solved, 0, j)
        at(14.05 + 0.01 * j, gather_first, 0, 1, j)
        for q in range(2):
            m = q * CHUNKS + j
            at(14.0 + q + late, above, q, j)
            place = 14.15 + q + late + (TAIL if m == CHUNKS - 1 else 0.0)
            at(place, above_z, m)
            at(place + 0.12, above_merge, m)
            at(16.5 + 0.1 * m, above_end, m)
    at(0.5, swap_inverse)
    at(0.6, swap_rhs)
    for i in range(4):
        at(2.5 + 0.5 * i, swap_coupling, i)
        at(4.5 + 0.5 * i, swap_first, i)
    at(15.0 + 0.1 * CHUNKS, forces_core)
    at(16.0, forces_z)
    at(17.0, forces_end)
    for _, _, step in sorted(plan, key=lambda item: (item[0], item[1])):
        step()
    assert not pending and len(sent) <= N_SEMS
    for copy in sent:
        copy.wait_send()


def body(inverse, coupling, panel, modes, rhs_window, rhs_above):
    n, w = CHUNKS, HALF // CHUNKS
    vmem = pl.BlockSpec(memory_space=pltpu.VMEM)

    def buf(*shape):
        return pltpu.VMEM(shape, BF16)

    return tuple(pl.pallas_call(
        kernel,
        out_shape=(
            jax.ShapeDtypeStruct((2, 16, 1024), BF16),
            jax.ShapeDtypeStruct((192, 1024), F32),
            jax.ShapeDtypeStruct((2, 1024), F32),
        ),
        in_specs=[pl.BlockSpec(memory_space=pl.ANY)] * 6,
        out_specs=(vmem,) * 3,
        scratch_shapes=[
            buf(2, n, 2, 4, 2, 16, w),
            buf(2, n, 2, 4, 4, 16, w),
            buf(2, n, 3, 2, 4, 16, w),
            buf(2, n, 2, 4, 16, w),
            buf(2, n, 3, 2, 16, w),
            buf(2, 2, n, 2, 4, 4, 16, w),
            buf(n, 2, 4, 2, 16, w),
            buf(n, 2, 4, 16, w),
            buf(n, 2, 4, 16, w),
            buf(n, 3, 2, 16, w),
            buf(2 * n, 4, 2, 192, w),
            buf(2 * n, 4, 192, w),
            buf(2 * n, 4, 192, w),
            buf(2 * n, 3, 192, w),
            pltpu.VMEM((16, 1024), F32),
            pltpu.VMEM((128, 128), F32),
            buf(4, 2, 16, 128),
            buf(4, 16, 128),
            buf(4, 16, 128),
            buf(3, 16, 128),
            pltpu.VMEM((16, 128), F32),
            buf(2, 2, 512, 128),
            buf(2, 128, 512),
            buf(2, 1536, 512),
            buf(2, 16, 512),
            buf(2, 16, 1024),
            buf(192, 1024),
            buf(16, HALF),
            pltpu.SemaphoreType.DMA((7,)),
            pltpu.SemaphoreType.DMA((N_SEMS,)),
            pltpu.SemaphoreType.DMA((N_SEMS,)),
            buf(2 * n, 192, w),
            pltpu.SemaphoreType.DMA((2 * n, 3)),
            pltpu.SemaphoreType.DMA((2 * n, 4)),
        ],
        compiler_params=pltpu.CompilerParams(
            collective_id=0, has_side_effects=True, vmem_limit_bytes=60 * 2**20
        ),
        cost_estimate=pl.CostEstimate(
            flops=3_700_000_000, bytes_accessed=6_000_000, transcendentals=0
        ),
    )(inverse, coupling, panel, modes, rhs_window, rhs_above))


def solution(mesh):
    placed = (
        P(None, "pcol", "prow"),
        P("prow", "pcol"),
        P(None, "prow", "pcol"),
        P(None, "prow", "pcol"),
        P(None, ("prow", "pcol"), None),
        P(("prow", "pcol"), None),
    )
    return jax.shard_map(
        body,
        mesh=mesh,
        in_specs=placed,
        out_specs=(
            P(None, ("pcol", "prow"), None),
            P(("prow", "pcol"), None),
            P(("prow", "pcol"), None),
        ),
        check_vma=False,
    )
```

```python
import functools

import jax
import jax.numpy as jnp
from jax import lax
from jax.experimental import pallas as pl
from jax.experimental.pallas import tpu as pltpu
from jax.sharding import PartitionSpec as P

MESH = pl.DeviceIdType.MESH
CHUNKS = 2
HALF = 512
TAIL = 0.8
PIECES = 16
PLACES = (2.3, 2.3, 2.3, 3.3, 3.3, 3.3, 5.3, 5.3, 5.3, 10.3, 10.3, 10.3, 11.3, 11.3, 12.3, 12.3)
N_SEMS = 200
BF16 = jnp.bfloat16
F32 = jnp.float32


def kernel(
    inv_hbm, coup_hbm, panel_hbm, modes_hbm, rhsw_hbm, rhsa_hbm,
    pot_ref, above_ref, forces_ref,
    g, part, r1, part2, r2, xs, cpart, cr1, cp2, cr2,
    fpart, fr1, fp2, fr2, fo, fot, fob, fob1, fo2, fo2r, fin,
    inv2, coup2, panel_ref, modes_ref, rhsw_ref, rhsa_ref, rw0,
    load_sems, send_sems, recv_sems, fm, f2_send, f2_recv, ps_send, ps_recv,
):
    w = g.shape[-1]
    row = lax.axis_index("prow")
    col = lax.axis_index("pcol")
    h, x, y = row // 16, (row // 4) % 4, row % 4
    zl, k = col // 2, col % 2

    loads = {}
    for name, src, dst in (
        ("rhsw", rhsw_hbm, rhsw_ref),
        ("inv1", inv_hbm.at[1], inv2.at[1, h]),
        ("coup", coup_hbm, coup2.at[h]),
        ("inv0", inv_hbm.at[0], inv2.at[0, h]),
        ("modes", modes_hbm, modes_ref),
        ("rhsa", rhsa_hbm, rhsa_ref),
    ):
        loads[name] = pltpu.make_async_copy(src, dst, load_sems.at[len(loads)])
        loads[name].start()

    ends = jnp.logical_or(zl == 0, zl == 3)
    kept = pl.ds(pl.multiple_of((zl // 3) * 384, 128), 1152)
    end_load = pltpu.make_async_copy(panel_hbm.at[:, kept], panel_ref.at[:, kept], load_sems.at[6])
    full_load = pltpu.make_async_copy(panel_hbm, panel_ref, load_sems.at[6])
    pl.when(ends)(end_load.start)
    pl.when(jnp.logical_not(ends))(full_load.start)

    def loaded(*names):
        for name in names:
            if name in loads:
                loads.pop(name).wait()

    def at_x(d):
        return (h * 16 + ((x + d) % 4) * 4 + y, col)

    def at_y(d):
        return (h * 16 + x * 4 + (y + d) % 4, col)

    def at_z(d):
        return (row, ((zl + d) % 4) * 2 + k)

    outer = jnp.logical_or(zl == 0, zl == 3)
    near = jnp.where(zl < 2, 1 - zl, 5 - zl)
    far = 3 - near

    def across_h(d):
        return ((1 - h) * 16 + x * 4 + y, ((zl + d) % 4) * 2 + k)

    other_row = (1 - h) * 16 + x * 4 + y
    at_h = ((1 - h) * 16 + x * 4 + y, col)
    sibling = (row, zl * 2 + 1 - k)

    barrier = pltpu.get_barrier_semaphore()
    partners = [at_x(d) for d in (1, 2, 3)] + [at_y(d) for d in (1, 2, 3)]
    partners += [at_z(d) for d in (1, 2, 3)] + [at_h, sibling]
    partners += [across_h(d) for d in (1, 2, 3)]
    for partner in partners:
        pl.semaphore_signal(barrier, inc=1, device_id=partner, device_id_type=MESH)
    pl.semaphore_wait(barrier, len(partners))

    sent = []
    pending = {}

    def send(key, src, dst, device):
        i = len(sent)
        copy = pltpu.make_async_remote_copy(
            src_ref=src, dst_ref=dst, send_sem=send_sems.at[i], recv_sem=recv_sems.at[i],
            device_id=device, device_id_type=MESH,
        )
        copy.start()
        sent.append(copy)
        pending.setdefault(key, []).append(copy)

    def arrived(key):
        for copy in pending.pop(key, ()):
            copy.wait_recv()

    def cols(half, j):
        return pl.ds(pl.multiple_of(half * HALF + j * w, 128), w)

    def first_axis(j):
        return "y" if j % 2 == 0 else "x"

    def load_rhs(j):
        loaded("rhsw")
        g[1, j, h, zl, k] = rhsw_ref[1, :, cols(h, j)]
        mine = g.at[1, j, h, zl, k]
        for d in (1, 2, 3):
            send(("gz", 1, j), mine, mine, at_z(d))
        for d in range(4):
            send(("gz", 1, j), rhsw_ref.at[1, :, cols(1 - h, j)], mine, across_h(d))

    def swap_inverse():
        send("inv1", inv_hbm.at[1], inv2.at[1, h], at_h)

    def swap_rhs():
        send("rw0", rhsw_ref.at[0, :, pl.ds(pl.multiple_of((1 - h) * HALF, 128), HALF)], rw0, at_h)

    def swap_coupling(part_no):
        rows = pl.ds(part_no * 32, 32)
        send("coup", coup_hbm.at[rows], coup2.at[h, rows], at_h)

    def panel_copy(piece):
        count = 768 // PIECES
        first = (piece * count) % 384
        rows = pl.ds(pl.multiple_of((3 - zl) * 384 + first, 16), count)
        return pltpu.make_async_remote_copy(
            src_ref=panel_hbm.at[piece * count // 384, rows], dst_ref=panel_ref.at[piece * count // 384, rows],
            send_sem=ps_send.at[piece], recv_sem=ps_recv.at[piece], device_id=at_h, device_id_type=MESH,
        )

    def swap_panel(piece):
        pl.when(outer)(panel_copy(piece).start)

    def swap_first(part_no):
        rows = pl.ds(part_no * 128, 128)
        send("inv0", inv_hbm.at[0, rows], inv2.at[0, h, rows], at_h)

    def gather_z(j):
        for d in (1, 2, 3):
            send(("gz", 0, j), g.at[0, j, :, zl, k], g.at[0, j, :, zl, k], at_z(d))

    def gather_core(b, j):
        arrived(("gz", b, j))
        send(("gc", b, j), g.at[b, j, :, :, k], g.at[b, j, :, :, k], sibling)

    def solve(b, j):
        loaded("inv%d" % b)
        arrived("inv%d" % b)
        arrived(("gc", b, j))
        right = g[b, j].reshape(2, 128, w)

        def tile(t, carry):
            rows = pl.ds(pl.multiple_of(t * 128, 128), 128)
            value = jnp.dot(inv2[b, 0, rows, :], right[0], preferred_element_type=F32)
            value += jnp.dot(inv2[b, 1, rows, :], right[1], preferred_element_type=F32)
            part[b, j, t // 2, pl.ds((t % 2) * 2, 2)] = value.astype(BF16).reshape(2, 4, 16, w)
            return carry

        lax.fori_loop(0, 4, tile, 0)
        for d in (1, 2, 3):
            if first_axis(j) == "y":
                send(("r1", b, j), part.at[b, j, :, :, (y + d) % 4], r1.at[b, j, d - 1], at_y(d))
            else:
                send(("r1", b, j), part.at[b, j, :, (x + d) % 4], r1.at[b, j, d - 1], at_x(d))

    def reduce_second(b, j):
        arrived(("r1", b, j))
        own = part[b, j, :, :, y] if first_axis(j) == "y" else part[b, j, :, x]
        total = own.astype(F32) + r1[b, j, 0].astype(F32)
        total = total + r1[b, j, 1].astype(F32) + r1[b, j, 2].astype(F32)
        part2[b, j] = total.astype(BF16)
        for d in (1, 2, 3):
            if first_axis(j) == "y":
                send(("r2", b, j), part2.at[b, j, :, (x + d) % 4], r2.at[b, j, d - 1], at_x(d))
            else:
                send(("r2", b, j), part2.at[b, j, :, (y + d) % 4], r2.at[b, j, d - 1], at_y(d))

    def spread_second(b, half, q, j):
        block = xs.at[b, half, j, :, x, y]
        for d in (1, 2, 3):
            send(("g2", b, q, j), block, block, at_x(d) if first_axis(j) == "y" else at_y(d))

    def solved(b, j):
        arrived(("r2", b, j))
        own = part2[b, j, :, x] if first_axis(j) == "y" else part2[b, j, :, y]
        total = own.astype(F32) + r2[b, j, 0].astype(F32)
        total = total + r2[b, j, 1].astype(F32) + r2[b, j, 2].astype(F32)
        xs[b, h, j, :, x, y] = total.astype(BF16)
        block = xs.at[b, h, j, :, x, y]
        if b == 0:
            send(("hh", b, j), block, block, at_h)
        spread_second(b, h, 0, j)
        if b == 1:
            send(("hh", b, j), block, block, at_h)
        pot_ref[b, :, cols(h, j)] = xs[b, h, j, h, x, y]

    def other_solved(b, j):
        arrived(("hh", b, j))
        spread_second(b, 1 - h, 1, j)
        pot_ref[b, :, cols(1 - h, j)] = xs[b, 1 - h, j, h, x, y]

    def gather_first(b, q, j):
        arrived(("g2", b, q, j))
        half = h if q == 0 else 1 - h
        for d in (1, 2, 3):
            if first_axis(j) == "y":
                block = xs.at[b, half, j, :, :, y]
                send(("g1", b, q, j), block, block, at_y(d))
            else:
                block = xs.at[b, half, j, :, x]
                send(("g1", b, q, j), block, block, at_x(d))

    def couple(j):
        loaded("coup")
        arrived("coup")
        arrived(("g1", 1, 0, j))
        right = xs[1, h, j].reshape(512, w)
        for side in range(2):
            value = jnp.dot(coup2[side], right, preferred_element_type=F32)
            cpart[j, side] = value.astype(BF16).reshape(4, 2, 16, w)
        send(("c1", j), cpart.at[j, :, :, 1 - k], cr1.at[j], sibling)

    def couple_z(j):
        arrived(("c1", j))
        cp2[j] = (cpart[j, :, :, k].astype(F32) + cr1[j].astype(F32)).astype(BF16)
        for d in (1, 2, 3):
            send(("c2", j), cp2.at[j, :, (zl + d) % 4], cr2.at[j, d - 1], at_z(d))

    def reduced(j):
        arrived(("c2", j))
        arrived("rw0")
        for side, rhs in ((h, rhsw_ref[0, :, cols(h, j)]), (1 - h, rw0[:, pl.ds(j * w, w)])):
            carried = cp2[j, side, zl].astype(F32) + cr2[j, 0, side].astype(F32)
            carried = carried + cr2[j, 1, side].astype(F32) + cr2[j, 2, side].astype(F32)
            g[0, j, side, zl, k] = (rhs.astype(F32) - carried).astype(BF16)
        gather_z(j)

    def above(q, i):
        j = q * CHUNKS + i
        half = h if q == 0 else 1 - h
        loaded("modes")
        if j == 0:
            pl.when(outer)(end_load.wait)
            pl.when(jnp.logical_not(outer))(full_load.wait)

            @pl.when(outer)
            def _():
                for piece in range(PIECES):
                    panel_copy(piece).wait_recv()

        arrived(("g1", 1, q, i))
        arrived(("g1", 0, q, i))

        def tile(t, carry):
            rows = pl.ds(pl.multiple_of(t * 192, 192), 192)
            value = jnp.dot(panel_ref[0, rows, :], xs[0, half, i].reshape(512, w), preferred_element_type=F32)
            value += jnp.dot(panel_ref[1, rows, :], xs[1, half, i].reshape(512, w), preferred_element_type=F32)
            fpart[j, t // 2, t % 2] = value.astype(BF16)
            return carry

        lax.fori_loop(0, 8, tile, 0)
        send(("f1", j), fpart.at[j, :, 1 - k], fr1.at[j], sibling)
        value = jnp.dot(modes_ref[0], xs[0, half, i].reshape(512, w), preferred_element_type=F32)
        value += jnp.dot(modes_ref[1], xs[1, half, i].reshape(512, w), preferred_element_type=F32)
        fo[:, cols(half, i)] = value

    def above_z(j):
        there = (j + CHUNKS) % (2 * CHUNKS)
        arrived(("f1", j))

        def tile(t, carry):
            fp2[j, t] = (fpart[j, t, k].astype(F32) + fr1[j, t].astype(F32)).astype(BF16)
            return carry

        lax.fori_loop(0, 4, tile, 0)
        @pl.when(outer)
        def _():
            f2_copy(j, 1, fp2.at[j, far], fm.at[j], 3, row, near).start()
            f2_copy(j, 2, fp2.at[j, near], fr2.at[j, 1], 1, row, near).start()
            f2_copy(j, 0, fp2.at[j, 3 - zl], fr2.at[there, 2], 2, other_row, 3 - zl, there).start()

        @pl.when(jnp.logical_not(outer))
        def _():
            f2_copy(j, 2, fp2.at[j, far], fr2.at[j, 1], 1, row, far).start()
            f2_copy(j, 1, fp2.at[j, near], fr2.at[j, 0], 0, row, near).start()
            fr2[j, 2] = jnp.zeros_like(fr2[j, 2])

    def f2_copy(j, slot, src, dst, landing, to_row, line, there=None):
        there = j if there is None else there
        return pltpu.make_async_remote_copy(
            src_ref=src, dst_ref=dst, send_sem=f2_send.at[j, slot], recv_sem=f2_recv.at[there, landing],
            device_id=(to_row, line * 2 + k), device_id_type=MESH,
        )

    def above_merge(j):
        @pl.when(jnp.logical_not(outer))
        def _():
            f2_copy(j, 0, fp2.at[j, far], fm.at[j], 3, row, near).wait_recv()
            merged = fp2[j, 3 - zl].astype(F32) + fm[j].astype(F32)
            fp2[j, 3 - zl] = merged.astype(BF16)
            f2_copy(j, 0, fp2.at[j, 3 - zl], fr2.at[j, 0], 0, row, 3 - zl).start()

    def above_end(j):
        loaded("rhsa")
        f2_copy(j, 0, fp2.at[j, zl], fr2.at[j, 0], 0, row, near).wait_recv()
        f2_copy(j, 0, fp2.at[j, zl], fr2.at[j, 1], 1, row, near).wait_recv()

        @pl.when(outer)
        def _():
            f2_copy(j, 0, fp2.at[j, zl], fr2.at[j, 2], 2, row, near).wait_recv()

        total = fp2[j, zl].astype(F32) + fr2[j, 0].astype(F32)
        total = total + fr2[j, 1].astype(F32) + fr2[j, 2].astype(F32)
        here = cols(h if j < CHUNKS else 1 - h, j % CHUNKS)
        above_ref[:, here] = rhsa_ref[:, here].astype(F32) - total
        for slot in range(3):
            f2_copy(j, slot, fp2.at[j, zl], fr2.at[j, 0], 0, row, near).wait_send()

    def forces_core():
        for m in range(16):
            for n in range(8):
                fot[pl.ds(m * 8 + n, 1), :] = fo[pl.ds(m, 1), pl.ds(n * 128, 128)]
        fob[...] = fot[...].astype(BF16).reshape(4, 2, 16, 128)
        send("o1", fob.at[:, 1 - k], fob1, sibling)

    def forces_z():
        arrived("o1")
        fo2[...] = (fob[:, k].astype(F32) + fob1[...].astype(F32)).astype(BF16)
        for d in (1, 2, 3):
            send("o2", fo2.at[(zl + d) % 4], fo2r.at[d - 1], at_z(d))

    def forces_end():
        arrived("o2")
        total = fo2[zl].astype(F32) + fo2r[0].astype(F32)
        fin[...] = total + fo2r[1].astype(F32) + fo2r[2].astype(F32)
        for m in range(2):
            for n in range(8):
                forces_ref[pl.ds(m, 1), pl.ds(n * 128, 128)] = fin[pl.ds(m * 8 + n, 1), :]

    plan = []

    def at(place, step, *args):
        plan.append((place, len(plan), functools.partial(step, *args)))

    for j in range(CHUNKS):
        late = 0.1 * j
        at(0.0 + late, load_rhs, j)
        at(1.0 + late, gather_core, 1, j)
        at(2.0 + late, solve, 1, j)
        at(3.0 + late, reduce_second, 1, j)
        at(4.0 + late, solved, 1, j)
        at(5.0 + late, gather_first, 1, 0, j)
        at(6.0 + late, couple, j)
        at(6.5 + late, other_solved, 1, j)
        at(7.0 + late, couple_z, j)
        at(7.5 + late, gather_first, 1, 1, j)
        at(8.0 + late, reduced, j)
        at(9.0 + late, gather_core, 0, j)
        at(10.0 + late, solve, 0, j)
        at(11.0 + late, reduce_second, 0, j)
        at(12.0 + late, solved, 0, j)
        at(13.0 + late, gather_first, 0, 0, j)
        at(13.5 + late, other_solved, 0, j)
        at(14.05 + 0.01 * j, gather_first, 0, 1, j)
        for q in range(2):
            m = q * CHUNKS + j
            at(14.0 + q + late, above, q, j)
            place = 14.15 + q + late + (TAIL if m == CHUNKS - 1 else 0.0)
            at(place, above_z, m)
            at(place + 0.12, above_merge, m)
            at(16.5 + 0.1 * m, above_end, m)
    at(0.5, swap_inverse)
    at(0.6, swap_rhs)
    for i in range(4):
        at(2.5 + 0.5 * i, swap_coupling, i)
        at(4.5 + 0.5 * i, swap_first, i)
    for i in range(PIECES):
        at(PLACES[i], swap_panel, i)
    at(15.0 + 0.1 * CHUNKS, forces_core)
    at(16.0, forces_z)
    at(17.0, forces_end)
    for _, _, step in sorted(plan, key=lambda item: (item[0], item[1])):
        step()
    assert not pending and len(sent) <= N_SEMS
    for copy in sent:
        copy.wait_send()

    @pl.when(outer)
    def _():
        for piece in range(PIECES):
            panel_copy(piece).wait_send()


def body(inverse, coupling, panel, modes, rhs_window, rhs_above):
    n, w = CHUNKS, HALF // CHUNKS
    vmem = pl.BlockSpec(memory_space=pltpu.VMEM)

    def buf(*shape):
        return pltpu.VMEM(shape, BF16)

    return tuple(pl.pallas_call(
        kernel,
        out_shape=(
            jax.ShapeDtypeStruct((2, 16, 1024), BF16),
            jax.ShapeDtypeStruct((192, 1024), F32),
            jax.ShapeDtypeStruct((2, 1024), F32),
        ),
        in_specs=[pl.BlockSpec(memory_space=pl.ANY)] * 6,
        out_specs=(vmem,) * 3,
        scratch_shapes=[
            buf(2, n, 2, 4, 2, 16, w),
            buf(2, n, 2, 4, 4, 16, w),
            buf(2, n, 3, 2, 4, 16, w),
            buf(2, n, 2, 4, 16, w),
            buf(2, n, 3, 2, 16, w),
            buf(2, 2, n, 2, 4, 4, 16, w),
            buf(n, 2, 4, 2, 16, w),
            buf(n, 2, 4, 16, w),
            buf(n, 2, 4, 16, w),
            buf(n, 3, 2, 16, w),
            buf(2 * n, 4, 2, 192, w),
            buf(2 * n, 4, 192, w),
            buf(2 * n, 4, 192, w),
            buf(2 * n, 3, 192, w),
            pltpu.VMEM((16, 1024), F32),
            pltpu.VMEM((128, 128), F32),
            buf(4, 2, 16, 128),
            buf(4, 16, 128),
            buf(4, 16, 128),
            buf(3, 16, 128),
            pltpu.VMEM((16, 128), F32),
            buf(2, 2, 512, 128),
            buf(2, 128, 512),
            buf(2, 1536, 512),
            buf(2, 16, 512),
            buf(2, 16, 1024),
            buf(192, 1024),
            buf(16, HALF),
            pltpu.SemaphoreType.DMA((7,)),
            pltpu.SemaphoreType.DMA((N_SEMS,)),
            pltpu.SemaphoreType.DMA((N_SEMS,)),
            buf(2 * n, 192, w),
            pltpu.SemaphoreType.DMA((2 * n, 3)),
            pltpu.SemaphoreType.DMA((2 * n, 4)),
            pltpu.SemaphoreType.DMA((PIECES,)),
            pltpu.SemaphoreType.DMA((PIECES,)),
        ],
        compiler_params=pltpu.CompilerParams(
            collective_id=0, has_side_effects=True, vmem_limit_bytes=60 * 2**20
        ),
        cost_estimate=pl.CostEstimate(
            flops=3_700_000_000, bytes_accessed=6_000_000, transcendentals=0
        ),
    )(inverse, coupling, panel, modes, rhs_window, rhs_above))


def solution(mesh):
    placed = (
        P(None, "pcol", "prow"),
        P("prow", "pcol"),
        P(None, "prow", "pcol"),
        P(None, "prow", "pcol"),
        P(None, ("prow", "pcol"), None),
        P(("prow", "pcol"), None),
    )
    return jax.shard_map(
        body,
        mesh=mesh,
        in_specs=placed,
        out_specs=(
            P(None, ("pcol", "prow"), None),
            P(("prow", "pcol"), None),
            P(("prow", "pcol"), None),
        ),
        check_vma=False,
    )
```

```python
import functools

import jax
import jax.numpy as jnp
from jax import lax
from jax.experimental import pallas as pl
from jax.experimental.pallas import tpu as pltpu
from jax.sharding import PartitionSpec as P

MESH = pl.DeviceIdType.MESH
CHUNKS = 2
HALF = 512
TAIL = 0.8
PIECES = 16
PLACES = (2.3, 2.3, 2.3, 3.3, 3.3, 3.3, 5.3, 5.3, 5.3, 10.3, 10.3, 10.3, 11.3, 11.3, 12.3, 12.3)
N_SEMS = 200
BF16 = jnp.bfloat16
F32 = jnp.float32


def kernel(
    inv_hbm, coup_hbm, panel_hbm, modes_hbm, rhsw_hbm, rhsa_hbm,
    pot_ref, above_ref, forces_ref,
    g, part, r1, part2, r2, xs, cpart, cr1, cp2, cr2,
    fpart, fr1, fp2, fr2, fo, fot, fob, fob1, fo2, fo2r, fin,
    inv2, coup2, panel_ref, modes_ref, rhsw_ref, rhsa_ref, rw0,
    load_sems, send_sems, recv_sems, fm, f2_send, f2_recv, ps_send, ps_recv,
):
    w = g.shape[-1]
    row = lax.axis_index("prow")
    col = lax.axis_index("pcol")
    h, x, y = row // 16, (row // 4) % 4, row % 4
    zl, k = col // 2, col % 2

    loads = {}
    for name, src, dst in (
        ("rhsw", rhsw_hbm, rhsw_ref),
        ("inv1", inv_hbm.at[1], inv2.at[1, h]),
        ("coup", coup_hbm, coup2.at[h]),
        ("inv0", inv_hbm.at[0], inv2.at[0, h]),
        ("modes", modes_hbm, modes_ref),
        ("rhsa", rhsa_hbm, rhsa_ref),
    ):
        loads[name] = pltpu.make_async_copy(src, dst, load_sems.at[len(loads)])
        loads[name].start()

    ends = jnp.logical_or(zl == 0, zl == 3)
    kept = pl.ds(pl.multiple_of((zl // 3) * 384, 128), 1152)
    end_load = pltpu.make_async_copy(panel_hbm.at[:, kept], panel_ref.at[:, kept], load_sems.at[6])
    full_load = pltpu.make_async_copy(panel_hbm, panel_ref, load_sems.at[6])
    pl.when(ends)(end_load.start)
    pl.when(jnp.logical_not(ends))(full_load.start)

    def loaded(*names):
        for name in names:
            if name in loads:
                loads.pop(name).wait()

    def at_x(d):
        return (h * 16 + ((x + d) % 4) * 4 + y, col)

    def at_y(d):
        return (h * 16 + x * 4 + (y + d) % 4, col)

    def at_z(d):
        return (row, ((zl + d) % 4) * 2 + k)

    outer = jnp.logical_or(zl == 0, zl == 3)
    near = jnp.where(zl < 2, 1 - zl, 5 - zl)
    far = 3 - near

    def across_h(d):
        return ((1 - h) * 16 + x * 4 + y, ((zl + d) % 4) * 2 + k)

    other_row = (1 - h) * 16 + x * 4 + y
    at_h = ((1 - h) * 16 + x * 4 + y, col)
    sibling = (row, zl * 2 + 1 - k)

    barrier = pltpu.get_barrier_semaphore()
    partners = [at_x(d) for d in (1, 2, 3)] + [at_y(d) for d in (1, 2, 3)]
    partners += [at_z(d) for d in (1, 2, 3)] + [at_h, sibling]
    partners += [across_h(d) for d in (1, 2, 3)]
    for partner in partners:
        pl.semaphore_signal(barrier, inc=1, device_id=partner, device_id_type=MESH)
    pl.semaphore_wait(barrier, len(partners))

    sent = []
    pending = {}

    def send(key, src, dst, device):
        i = len(sent)
        copy = pltpu.make_async_remote_copy(
            src_ref=src, dst_ref=dst, send_sem=send_sems.at[i], recv_sem=recv_sems.at[i],
            device_id=device, device_id_type=MESH,
        )
        copy.start()
        sent.append(copy)
        pending.setdefault(key, []).append(copy)

    def arrived(key):
        for copy in pending.pop(key, ()):
            copy.wait_recv()

    def cols(half, j):
        return pl.ds(pl.multiple_of(half * HALF + j * w, 128), w)

    def first_axis(j):
        return "y" if j % 2 == 0 else "x"

    def load_rhs(j):
        loaded("rhsw")
        g[1, j, h, zl, k] = rhsw_ref[1, :, cols(h, j)]
        mine = g.at[1, j, h, zl, k]
        for d in (1, 2, 3):
            send(("gz", 1, j), mine, mine, at_z(d))
        for d in range(4):
            send(("gz", 1, j), rhsw_ref.at[1, :, cols(1 - h, j)], mine, across_h(d))

    def swap_inverse():
        send("inv1", inv_hbm.at[1], inv2.at[1, h], at_h)

    def swap_rhs():
        send("rw0", rhsw_ref.at[0, :, pl.ds(pl.multiple_of((1 - h) * HALF, 128), HALF)], rw0, at_h)

    def swap_coupling(part_no):
        rows = pl.ds(part_no * 32, 32)
        send("coup", coup_hbm.at[rows], coup2.at[h, rows], at_h)

    def panel_copy(piece):
        count = 768 // PIECES
        first = (piece * count) % 384
        rows = pl.ds(pl.multiple_of((3 - zl) * 384 + first, 16), count)
        return pltpu.make_async_remote_copy(
            src_ref=panel_hbm.at[piece * count // 384, rows], dst_ref=panel_ref.at[piece * count // 384, rows],
            send_sem=ps_send.at[piece], recv_sem=ps_recv.at[piece], device_id=at_h, device_id_type=MESH,
        )

    def swap_panel(piece):
        pl.when(outer)(panel_copy(piece).start)

    def swap_first(part_no):
        rows = pl.ds(part_no * 128, 128)
        send("inv0", inv_hbm.at[0, rows], inv2.at[0, h, rows], at_h)

    def gather_z(j):
        for d in (1, 2, 3):
            send(("gz", 0, j), g.at[0, j, :, zl, k], g.at[0, j, :, zl, k], at_z(d))

    def gather_core(b, j):
        arrived(("gz", b, j))
        send(("gc", b, j), g.at[b, j, :, :, k], g.at[b, j, :, :, k], sibling)

    def solve(b, j):
        loaded("inv%d" % b)
        arrived("inv%d" % b)
        arrived(("gc", b, j))
        right = g[b, j].reshape(2, 128, w)

        def tile(t, carry):
            rows = pl.ds(pl.multiple_of(t * 128, 128), 128)
            value = jnp.dot(inv2[b, 0, rows, :], right[0], preferred_element_type=F32)
            value += jnp.dot(inv2[b, 1, rows, :], right[1], preferred_element_type=F32)
            part[b, j, t // 2, pl.ds((t % 2) * 2, 2)] = value.astype(BF16).reshape(2, 4, 16, w)
            return carry

        lax.fori_loop(0, 4, tile, 0)
        for d in (1, 2, 3):
            if first_axis(j) == "y":
                send(("r1", b, j), part.at[b, j, :, :, (y + d) % 4], r1.at[b, j, d - 1], at_y(d))
            else:
                send(("r1", b, j), part.at[b, j, :, (x + d) % 4], r1.at[b, j, d - 1], at_x(d))

    def reduce_second(b, j):
        arrived(("r1", b, j))
        own = part[b, j, :, :, y] if first_axis(j) == "y" else part[b, j, :, x]
        total = own.astype(F32) + r1[b, j, 0].astype(F32)
        total = total + r1[b, j, 1].astype(F32) + r1[b, j, 2].astype(F32)
        part2[b, j] = total.astype(BF16)
        for d in (1, 2, 3):
            if first_axis(j) == "y":
                send(("r2", b, j), part2.at[b, j, :, (x + d) % 4], r2.at[b, j, d - 1], at_x(d))
            else:
                send(("r2", b, j), part2.at[b, j, :, (y + d) % 4], r2.at[b, j, d - 1], at_y(d))

    def spread_second(b, half, q, j):
        block = xs.at[b, half, j, :, x, y]
        for d in (1, 2, 3):
            send(("g2", b, q, j), block, block, at_x(d) if first_axis(j) == "y" else at_y(d))

    def solved(b, j):
        arrived(("r2", b, j))
        own = part2[b, j, :, x] if first_axis(j) == "y" else part2[b, j, :, y]
        total = own.astype(F32) + r2[b, j, 0].astype(F32)
        total = total + r2[b, j, 1].astype(F32) + r2[b, j, 2].astype(F32)
        xs[b, h, j, :, x, y] = total.astype(BF16)
        block = xs.at[b, h, j, :, x, y]
        if b == 0:
            send(("hh", b, j), block, block, at_h)
        spread_second(b, h, 0, j)
        if b == 1:
            send(("hh", b, j), block, block, at_h)
        pot_ref[b, :, cols(h, j)] = xs[b, h, j, h, x, y]

    def other_solved(b, j):
        arrived(("hh", b, j))
        spread_second(b, 1 - h, 1, j)
        pot_ref[b, :, cols(1 - h, j)] = xs[b, 1 - h, j, h, x, y]

    def gather_first(b, q, j):
        arrived(("g2", b, q, j))
        half = h if q == 0 else 1 - h
        for d in (1, 2, 3):
            if first_axis(j) == "y":
                block = xs.at[b, half, j, :, :, y]
                send(("g1", b, q, j), block, block, at_y(d))
            else:
                block = xs.at[b, half, j, :, x]
                send(("g1", b, q, j), block, block, at_x(d))

    def couple(j):
        loaded("coup")
        arrived("coup")
        arrived(("g1", 1, 0, j))
        right = xs[1, h, j].reshape(512, w)
        for side in range(2):
            value = jnp.dot(coup2[side], right, preferred_element_type=F32)
            cpart[j, side] = value.astype(BF16).reshape(4, 2, 16, w)
        send(("c1", j), cpart.at[j, :, :, 1 - k], cr1.at[j], sibling)

    def couple_z(j):
        arrived(("c1", j))
        cp2[j] = (cpart[j, :, :, k].astype(F32) + cr1[j].astype(F32)).astype(BF16)
        for d in (1, 2, 3):
            send(("c2", j), cp2.at[j, :, (zl + d) % 4], cr2.at[j, d - 1], at_z(d))

    def reduced(j):
        arrived(("c2", j))
        arrived("rw0")
        for side, rhs in ((h, rhsw_ref[0, :, cols(h, j)]), (1 - h, rw0[:, pl.ds(j * w, w)])):
            carried = cp2[j, side, zl].astype(F32) + cr2[j, 0, side].astype(F32)
            carried = carried + cr2[j, 1, side].astype(F32) + cr2[j, 2, side].astype(F32)
            g[0, j, side, zl, k] = (rhs.astype(F32) - carried).astype(BF16)
        gather_z(j)

    def above(q, i):
        j = q * CHUNKS + i
        half = h if q == 0 else 1 - h
        loaded("modes")
        if j == 0:
            pl.when(outer)(end_load.wait)
            pl.when(jnp.logical_not(outer))(full_load.wait)

            @pl.when(outer)
            def _():
                for piece in range(PIECES):
                    panel_copy(piece).wait_recv()

        arrived(("g1", 1, q, i))
        arrived(("g1", 0, q, i))

        def tile(t, carry):
            rows = pl.ds(pl.multiple_of(t * 192, 192), 192)
            value = jnp.dot(panel_ref[0, rows, :], xs[0, half, i].reshape(512, w), preferred_element_type=F32)
            value += jnp.dot(panel_ref[1, rows, :], xs[1, half, i].reshape(512, w), preferred_element_type=F32)
            fpart[j, t // 2, t % 2] = value.astype(BF16)
            return carry

        lax.fori_loop(0, 8, tile, 0)
        send(("f1", j), fpart.at[j, :, 1 - k], fr1.at[j], sibling)
        value = jnp.dot(modes_ref[0], xs[0, half, i].reshape(512, w), preferred_element_type=F32)
        value += jnp.dot(modes_ref[1], xs[1, half, i].reshape(512, w), preferred_element_type=F32)
        fo[:, cols(half, i)] = value

    def above_z(j):
        there = (j + CHUNKS) % (2 * CHUNKS)
        arrived(("f1", j))

        def add(t):
            fp2[j, t] = (fpart[j, t, k].astype(F32) + fr1[j, t].astype(F32)).astype(BF16)

        @pl.when(outer)
        def _():
            add(far)
            f2_copy(j, 1, fp2.at[j, far], fm.at[j], 3, row, near).start()
            add(near)
            f2_copy(j, 2, fp2.at[j, near], fr2.at[j, 1], 1, row, near).start()
            add(3 - zl)
            f2_copy(j, 0, fp2.at[j, 3 - zl], fr2.at[there, 2], 2, other_row, 3 - zl, there).start()

        @pl.when(jnp.logical_not(outer))
        def _():
            add(far)
            f2_copy(j, 2, fp2.at[j, far], fr2.at[j, 1], 1, row, far).start()
            add(near)
            f2_copy(j, 1, fp2.at[j, near], fr2.at[j, 0], 0, row, near).start()
            add(3 - zl)
            fr2[j, 2] = jnp.zeros_like(fr2[j, 2])
        add(zl)

    def f2_copy(j, slot, src, dst, landing, to_row, line, there=None):
        there = j if there is None else there
        return pltpu.make_async_remote_copy(
            src_ref=src, dst_ref=dst, send_sem=f2_send.at[j, slot], recv_sem=f2_recv.at[there, landing],
            device_id=(to_row, line * 2 + k), device_id_type=MESH,
        )

    def above_merge(j):
        @pl.when(jnp.logical_not(outer))
        def _():
            f2_copy(j, 0, fp2.at[j, far], fm.at[j], 3, row, near).wait_recv()
            merged = fp2[j, 3 - zl].astype(F32) + fm[j].astype(F32)
            fp2[j, 3 - zl] = merged.astype(BF16)
            f2_copy(j, 0, fp2.at[j, 3 - zl], fr2.at[j, 0], 0, row, 3 - zl).start()

    def above_end(j):
        loaded("rhsa")
        f2_copy(j, 0, fp2.at[j, zl], fr2.at[j, 0], 0, row, near).wait_recv()
        f2_copy(j, 0, fp2.at[j, zl], fr2.at[j, 1], 1, row, near).wait_recv()

        @pl.when(outer)
        def _():
            f2_copy(j, 0, fp2.at[j, zl], fr2.at[j, 2], 2, row, near).wait_recv()

        total = fp2[j, zl].astype(F32) + fr2[j, 0].astype(F32)
        total = total + fr2[j, 1].astype(F32) + fr2[j, 2].astype(F32)
        here = cols(h if j < CHUNKS else 1 - h, j % CHUNKS)
        above_ref[:, here] = rhsa_ref[:, here].astype(F32) - total
        for slot in range(3):
            f2_copy(j, slot, fp2.at[j, zl], fr2.at[j, 0], 0, row, near).wait_send()

    def forces_core():
        for m in range(16):
            for n in range(8):
                fot[pl.ds(m * 8 + n, 1), :] = fo[pl.ds(m, 1), pl.ds(n * 128, 128)]
        fob[...] = fot[...].astype(BF16).reshape(4, 2, 16, 128)
        send("o1", fob.at[:, 1 - k], fob1, sibling)

    def forces_z():
        arrived("o1")
        fo2[...] = (fob[:, k].astype(F32) + fob1[...].astype(F32)).astype(BF16)
        for d in (1, 2, 3):
            send("o2", fo2.at[(zl + d) % 4], fo2r.at[d - 1], at_z(d))

    def forces_end():
        arrived("o2")
        total = fo2[zl].astype(F32) + fo2r[0].astype(F32)
        fin[...] = total + fo2r[1].astype(F32) + fo2r[2].astype(F32)
        for m in range(2):
            for n in range(8):
                forces_ref[pl.ds(m, 1), pl.ds(n * 128, 128)] = fin[pl.ds(m * 8 + n, 1), :]

    plan = []

    def at(place, step, *args):
        plan.append((place, len(plan), functools.partial(step, *args)))

    for j in range(CHUNKS):
        late = 0.1 * j
        at(0.0 + late, load_rhs, j)
        at(1.0 + late, gather_core, 1, j)
        at(2.0 + late, solve, 1, j)
        at(3.0 + late, reduce_second, 1, j)
        at(4.0 + late, solved, 1, j)
        at(5.0 + late, gather_first, 1, 0, j)
        at(6.0 + late, couple, j)
        at(6.5 + late, other_solved, 1, j)
        at(7.0 + late, couple_z, j)
        at(7.5 + late, gather_first, 1, 1, j)
        at(8.0 + late, reduced, j)
        at(9.0 + late, gather_core, 0, j)
        at(10.0 + late, solve, 0, j)
        at(11.0 + late, reduce_second, 0, j)
        at(12.0 + late, solved, 0, j)
        at(13.0 + late, gather_first, 0, 0, j)
        at(13.5 + late, other_solved, 0, j)
        at(14.05 + 0.01 * j, gather_first, 0, 1, j)
        for q in range(2):
            m = q * CHUNKS + j
            at(14.0 + q + late, above, q, j)
            place = 14.15 + q + late + (TAIL if m == CHUNKS - 1 else 0.0)
            at(place, above_z, m)
            at(place + 0.12, above_merge, m)
            at(16.5 + 0.1 * m, above_end, m)
    at(0.5, swap_inverse)
    at(0.6, swap_rhs)
    for i in range(4):
        at(2.5 + 0.5 * i, swap_coupling, i)
        at(4.5 + 0.5 * i, swap_first, i)
    for i in range(PIECES):
        at(PLACES[i], swap_panel, i)
    at(15.12, forces_core)
    at(15.24, forces_z)
    at(17.0, forces_end)
    for _, _, step in sorted(plan, key=lambda item: (item[0], item[1])):
        step()
    assert not pending and len(sent) <= N_SEMS
    for copy in sent:
        copy.wait_send()

    @pl.when(outer)
    def _():
        for piece in range(PIECES):
            panel_copy(piece).wait_send()


def body(inverse, coupling, panel, modes, rhs_window, rhs_above):
    n, w = CHUNKS, HALF // CHUNKS
    vmem = pl.BlockSpec(memory_space=pltpu.VMEM)

    def buf(*shape):
        return pltpu.VMEM(shape, BF16)

    return tuple(pl.pallas_call(
        kernel,
        out_shape=(
            jax.ShapeDtypeStruct((2, 16, 1024), BF16),
            jax.ShapeDtypeStruct((192, 1024), F32),
            jax.ShapeDtypeStruct((2, 1024), F32),
        ),
        in_specs=[pl.BlockSpec(memory_space=pl.ANY)] * 6,
        out_specs=(vmem,) * 3,
        scratch_shapes=[
            buf(2, n, 2, 4, 2, 16, w),
            buf(2, n, 2, 4, 4, 16, w),
            buf(2, n, 3, 2, 4, 16, w),
            buf(2, n, 2, 4, 16, w),
            buf(2, n, 3, 2, 16, w),
            buf(2, 2, n, 2, 4, 4, 16, w),
            buf(n, 2, 4, 2, 16, w),
            buf(n, 2, 4, 16, w),
            buf(n, 2, 4, 16, w),
            buf(n, 3, 2, 16, w),
            buf(2 * n, 4, 2, 192, w),
            buf(2 * n, 4, 192, w),
            buf(2 * n, 4, 192, w),
            buf(2 * n, 3, 192, w),
            pltpu.VMEM((16, 1024), F32),
            pltpu.VMEM((128, 128), F32),
            buf(4, 2, 16, 128),
            buf(4, 16, 128),
            buf(4, 16, 128),
            buf(3, 16, 128),
            pltpu.VMEM((16, 128), F32),
            buf(2, 2, 512, 128),
            buf(2, 128, 512),
            buf(2, 1536, 512),
            buf(2, 16, 512),
            buf(2, 16, 1024),
            buf(192, 1024),
            buf(16, HALF),
            pltpu.SemaphoreType.DMA((7,)),
            pltpu.SemaphoreType.DMA((N_SEMS,)),
            pltpu.SemaphoreType.DMA((N_SEMS,)),
            buf(2 * n, 192, w),
            pltpu.SemaphoreType.DMA((2 * n, 3)),
            pltpu.SemaphoreType.DMA((2 * n, 4)),
            pltpu.SemaphoreType.DMA((PIECES,)),
            pltpu.SemaphoreType.DMA((PIECES,)),
        ],
        compiler_params=pltpu.CompilerParams(
            collective_id=0, has_side_effects=True, vmem_limit_bytes=60 * 2**20
        ),
        cost_estimate=pl.CostEstimate(
            flops=3_700_000_000, bytes_accessed=6_000_000, transcendentals=0
        ),
    )(inverse, coupling, panel, modes, rhs_window, rhs_above))


def solution(mesh):
    placed = (
        P(None, "pcol", "prow"),
        P("prow", "pcol"),
        P(None, "prow", "pcol"),
        P(None, "prow", "pcol"),
        P(None, ("prow", "pcol"), None),
        P(("prow", "pcol"), None),
    )
    return jax.shard_map(
        body,
        mesh=mesh,
        in_specs=placed,
        out_specs=(
            P(None, ("pcol", "prow"), None),
            P(("prow", "pcol"), None),
            P(("prow", "pcol"), None),
        ),
        check_vma=False,
    )
```
